32 devices in a mesh: section: 4 (over y, x), dp: 8 (over z, core).
Axes of the slice: x: 2, y: 2, z: 4, core: 2. Of those that a mesh axis runs over, the one named last changes fastest.
Arguments:
- inputs: bfloat16 [12288, 512], P('dp'), may hold values from -6 to 6
- weights: bfloat16 [120, 512, 512], P('section')
- biases: float32 [28, 512], P('section'), may hold values from -1.5 to 1.5
- gain_rows: float32 [8, 512], P('section'), may hold values from 0.5 to 1.5
- block_series: int32 [32, 8], P('dp'), may hold values from 0 to 7, as said below
- cotangent: bfloat16 [12288, 512], P('dp'), may hold values from -6 to 6
Outputs:
- layer_output: bfloat16 [12288, 512], P('dp', 'section')
- input_grad: float32 [12288, 512], P('dp', 'section')
- weight_grad: float32 [120, 512, 512], P('section')
- bias_grad: float32 [28, 512], P('section')
- gain_grad: float32 [8, 512], P('section')
The draws below stay inside these ranges and needn't reach their ends.
Inputs may be any that keep to these rules, and one draw needn't show every extreme that they name: block_series[b, k] numbers the series that holds block k (48 rows) of buffer b, where buffer b is micro-batch b % 4 of device b // 4 along dp: it is 0 for k = 0 and rises by 0 or 1 from one block to the next; every series holds 1 to 4 blocks, some series holds 4 blocks, and in some buffer the number reaches 7.
All inputs are finite; a program needn't handle non-finite values.
Results may differ from the reference program's by a relative error of at most 0.014.
Values may be sent and summed in bfloat16 or wider, within the bound.
No kernel may reach another device: no remote copies, remote signals or barrier semaphores. Data moves between devices by JAX's collectives and lax.ppermute only.
A program may use at most 832 MiB of HBM per device.

```python
import jax
import jax.numpy as jnp
from jax import lax

D = 512
FF = 2048
SCALE_A = 12
SCALE_B = 16
BLOCK = 48
LMAX = 192
HALF = 12
TAPS_A = 16
TAPS_B = 12
TILES = 30
BROWS = 7
GROWS = 2
ROWS = 384
MB_BLOCKS = 8
BUFFERS = 32
TOKENS = 12288
N_SECTION = 4


def draw_weights(key, part):
    key = jax.random.fold_in(key, 11)
    tile_index = jnp.arange(N_SECTION * TILES)
    section_index = tile_index // TILES
    position = tile_index % TILES
    channels = jnp.float32(D)
    first_fan = jnp.where(position < SCALE_A, SCALE_A * channels, SCALE_B * channels)
    second_fan = jnp.where(position < TAPS_A, TAPS_A * channels, TAPS_B * channels)
    third_fan = jnp.where(position < SCALE_A + SCALE_B, channels, 2.0 * channels)
    last_fan = jnp.where(position < FF // D, channels, jnp.where(position < 2 * (FF // D), 4.0 * channels, channels / 16.0))
    fan_in = jnp.where(section_index == 0, first_fan, jnp.where(section_index == 1, second_fan, jnp.where(section_index == 2, third_fan, last_fan)))
    factor = lax.rsqrt(fan_in)
    noise = jax.random.normal(key, (N_SECTION * TILES, D, D), jnp.float32)
    return (noise * factor[:, None, None]).astype(jnp.bfloat16)


def draw_block_series(key, part):
    key = jax.random.fold_in(key, 23)
    longest = LMAX // BLOCK
    spans = jax.random.randint(key, (BUFFERS, MB_BLOCKS), 1, longest + 1)
    chosen = jax.random.randint(jax.random.fold_in(key, 1), (), 0, BUFFERS)
    finest = (chosen + 1) % BUFFERS
    spans = jnp.where((jnp.arange(BUFFERS) == finest)[:, None], 1, spans)
    spans = spans.at[chosen, 0].set(longest)
    ends = jnp.cumsum(spans, axis=1)
    position = jnp.arange(MB_BLOCKS)
    return jnp.sum((ends[:, None, :] <= position[None, :, None]).astype(jnp.int32), axis=2)


def block_levels(rng, extent, shards, low, top_value):
    gain = 1.0
    for axis_at, blocks in shards:
        heights = jax.random.uniform(jax.random.fold_in(jax.random.fold_in(rng, 6), axis_at), (blocks,), jnp.float32, low / len(shards), top_value / len(shards))
        gain = gain * jnp.repeat(jnp.exp(heights), extent[axis_at] // blocks).reshape((-1,) + (1,) * (len(extent) - 1 - axis_at))
    return gain


def scatter_about(stream_key, dims, scale, reach, split=(), kind=jnp.bfloat16):
    level = block_levels(stream_key, dims, split, -0.22, 0.18) if split else 1.0
    result = jax.random.normal(stream_key, dims, jnp.float32) * scale * level
    return jnp.minimum(jnp.maximum(result, -reach), reach).astype(kind)


def setup_inputs(seed: int = 0) -> dict:
    keys = jax.random.split(jax.random.key(seed), 7)
    inputs = scatter_about(keys[0], (TOKENS, D), 1.0, 6.0, ((0, 8),))
    weights = draw_weights(jax.random.fold_in(keys[6], 71), 0)
    biases = scatter_about(keys[2], (N_SECTION * BROWS, D), 0.3, 1.5, ((0, 4),), jnp.float32)
    gain_rows = jnp.clip(1.0 + 0.1 * jax.random.normal(keys[3], (N_SECTION * GROWS, D), jnp.float32), 0.5, 1.5)
    block_series = draw_block_series(jax.random.fold_in(keys[6], 71), 0)
    cotangent = scatter_about(keys[5], (TOKENS, D), 1.0, 6.0, ((0, 8),))
    return dict(inputs=inputs, weights=weights, biases=biases, gain_rows=gain_rows, block_series=block_series, cotangent=cotangent)


@jax.custom_vjp
def low(v):
    return lax.optimization_barrier(v.astype(jnp.bfloat16)).astype(jnp.float32)

@jax.custom_vjp
def low_back(v):
    return v

def low_keep(v):
    return (low(v), None)

def low_pass(kept, grad):
    return (grad,)

def back_keep(v):
    return (v, None)

def back_low(kept, grad):
    return (low(grad),)
low.defvjp(low_keep, low_pass)
low_back.defvjp(back_keep, back_low)

def shift_rows(field_rows, offset, filler):
    if offset == 0:
        return field_rows
    row_count = field_rows.shape[0]
    padding = jnp.full((abs(offset),) + field_rows.shape[1:], filler, field_rows.dtype)
    if offset > 0:
        return jnp.concatenate([field_rows[offset:], padding], 0)
    return jnp.concatenate([padding, field_rows[:row_count + offset]], 0)

def masked_sum(field_rows, series):
    window_sum = jnp.zeros(field_rows.shape, jnp.float32)
    window_count = jnp.zeros((field_rows.shape[0], 1), jnp.float32)
    for offset in range(-HALF, HALF + 1):
        matches = (shift_rows(series, offset, -1) == series)[:, None]
        window_sum = window_sum + jnp.where(matches, shift_rows(field_rows, offset, 0.0), 0.0)
        window_count = window_count + matches.astype(jnp.float32)
    return (window_sum, window_count)

def layer_norm(values, gain_row, shift_row):
    centered = values - lax.optimization_barrier(jnp.mean(values, axis=-1, keepdims=True))
    variance = lax.optimization_barrier(jnp.mean(centered * centered, axis=-1, keepdims=True))
    return centered * lax.rsqrt(variance + 1e-05) * gain_row + shift_row

def exact_product(left_side, right_side):
    return jnp.dot(left_side, right_side, precision=lax.Precision.HIGHEST, preferred_element_type=jnp.float32)

def layer(feed_buffer, kernels, bias_table, gain_table, series):
    row_count, channels = feed_buffer.shape
    tiles = kernels.reshape(N_SECTION, TILES, channels, channels)
    bias_rows = bias_table.reshape(N_SECTION, BROWS, channels)
    gain_rows = gain_table.reshape(N_SECTION, GROWS, channels)
    window_sum, window_count = masked_sum(feed_buffer, series)
    trend_part = window_sum / window_count
    season_low = low(feed_buffer - trend_part)
    season_wire = low_back(season_low)
    strides = (SCALE_A, SCALE_B)
    tap_counts = (TAPS_A, TAPS_B)
    down_firsts = (0, SCALE_A)
    tap_firsts = (0, TAPS_A)
    iso_outs = []
    for member in range(2):
        stride = strides[member]
        kernel = tiles[0, down_firsts[member]:down_firsts[member] + stride].reshape(stride * channels, channels)
        pre_act = low_back(exact_product(season_low.reshape(row_count // stride, stride * channels), kernel) + bias_rows[0, member])
        coarse = low_back(low(jnp.tanh(pre_act)))
        coarse_series = series[::stride]
        iso_sum = jnp.zeros(coarse.shape, jnp.float32)
        for offset in range(tap_counts[member]):
            matches = (shift_rows(coarse_series, -offset, -1) == coarse_series)[:, None]
            moved = jnp.where(matches, shift_rows(coarse, -offset, 0.0), 0.0)
            iso_sum = iso_sum + exact_product(moved, tiles[1, tap_firsts[member] + offset])
        iso_pre = low_back(iso_sum + bias_rows[1, member])
        normed = layer_norm(jnp.tanh(iso_pre) + coarse, gain_rows[1, member], bias_rows[1, 2 + member])
        iso_outs.append(low_back(low(normed)))
    merged = bias_rows[2, 4]
    for member in range(2):
        stride = strides[member]
        kernel = tiles[2, down_firsts[member]:down_firsts[member] + stride]
        spread = jnp.einsum('pd,kde->pke', iso_outs[member], kernel, precision=lax.Precision.HIGHEST).reshape(row_count, channels)
        upward_pre = low_back(spread + bias_rows[2, member])
        upward_out = layer_norm(jnp.tanh(upward_pre) + season_wire, gain_rows[2, member], bias_rows[2, 2 + member])
        merged = merged + exact_product(low(upward_out), tiles[2, SCALE_A + SCALE_B + member])
    mixed_rows = low_back(low(merged))
    hidden_tiles = FF // D
    input_tiles = tiles[3, 0:hidden_tiles].transpose(1, 0, 2).reshape(channels, hidden_tiles * channels)
    hidden_pre = low_back(exact_product(mixed_rows, input_tiles) + bias_rows[3, 0:hidden_tiles].reshape(hidden_tiles * channels))
    activated = low(jax.nn.gelu(hidden_pre, approximate=False))
    output_tiles = tiles[3, hidden_tiles:2 * hidden_tiles].reshape(hidden_tiles * channels, channels)
    branch_out = low_back(exact_product(activated, output_tiles) + bias_rows[3, hidden_tiles])
    normed = layer_norm(mixed_rows + branch_out, gain_rows[3, 0], bias_rows[3, hidden_tiles + 1])
    return normed + exact_product(low(trend_part), tiles[3, 2 * hidden_tiles]) + bias_rows[3, hidden_tiles + 2]

def reference(inputs, weights, biases, gain_rows, block_series, cotangent):
    feed_rows = inputs.astype(jnp.float32).reshape(BUFFERS, ROWS, D)
    target_rows = cotangent.astype(jnp.float32).reshape(BUFFERS, ROWS, D)
    kernels = weights.astype(jnp.float32)
    series_rows = jnp.repeat(block_series, BLOCK, axis=1)

    def one_buffer(carried, buffer_item):
        feed_buffer, target, series = buffer_item

        def forward(feed_in, kernel_in, bias_in, gain_in):
            return layer(feed_in, kernel_in, bias_in, gain_in, series)
        layer_value, pullback = jax.vjp(forward, feed_buffer, kernels, biases, gain_rows)
        grad_feed, grad_kernel, grad_bias, grad_gain = pullback(target)
        summed = (carried[0] + grad_kernel, carried[1] + grad_bias, carried[2] + grad_gain)
        return (summed, (layer_value, grad_feed))
    start_sums = (jnp.zeros(kernels.shape, jnp.float32), jnp.zeros(biases.shape, jnp.float32), jnp.zeros(gain_rows.shape, jnp.float32))
    grad_sums, (layer_values, grad_feeds) = lax.scan(one_buffer, start_sums, (feed_rows, target_rows, series_rows))
    return (layer_values.reshape(TOKENS, D).astype(jnp.bfloat16), grad_feeds.reshape(TOKENS, D), grad_sums[0], grad_sums[1], grad_sums[2])
```

```python
import math

import jax
import jax.numpy as jnp
from jax import lax
from jax.experimental import pallas as pl
from jax.experimental.pallas import tpu as pltpu
from jax.sharding import PartitionSpec as P

D = 512
HIDDEN_TILES = 4
SCALE_A = 12
SCALE_B = 16
BLOCK = 48
HALF = 12
TAPS_A = 16
TAPS_B = 12
DOWN_TILES = SCALE_A + SCALE_B
SMALL_ROWS = 16
LANES = 128
COLS = D // LANES

F32 = jnp.float32
BF16 = jnp.bfloat16

STRIDES = (SCALE_A, SCALE_B)
FIRST_TILE = (0, SCALE_A)
TAPS = (TAPS_A, TAPS_B)
FIRST_TAP = (0, TAPS_A)


def mm(a, b):
    return jnp.dot(a, b, preferred_element_type=F32)


def mm_nt(a, b):
    return lax.dot_general(a, b, (((1,), (1,)), ((), ())), preferred_element_type=F32)


def mm_tn(a, b):
    return lax.dot_general(a, b, (((0,), (0,)), ((), ())), preferred_element_type=F32)


def row_mean(v):
    return jnp.mean(v, axis=-1, keepdims=True)


def col_sum(v):
    return jnp.sum(v, axis=0, keepdims=True)


def normal(v):
    centered = v - row_mean(v)
    scale = lax.rsqrt(row_mean(centered * centered) + 1e-05)
    return centered * scale, scale


def normal_back(o, gain, n, scale):
    og = o * gain
    return scale * (og - row_mean(og) - n * row_mean(og * n))


def spread_get(ref, lead, start, size, stride):
    return jnp.concatenate(
        [ref[lead + (c, pl.ds(start, size, stride=stride), slice(None))] for c in range(COLS)], 1
    )


def spread_set(ref, lead, start, size, stride, value):
    for c in range(COLS):
        ref[lead + (c, pl.ds(start, size, stride=stride), slice(None))] = value[
            :, c * LANES : (c + 1) * LANES
        ]


def block_get(ref, lead, start, size):
    return jnp.concatenate(
        [ref[lead + (c, pl.ds(start, size), slice(None))] for c in range(COLS)], 1
    )


def block_set(ref, lead, start, size, value):
    for c in range(COLS):
        ref[lead + (c, pl.ds(start, size), slice(None))] = value[:, c * LANES : (c + 1) * LANES]


def window_of(col, row):
    size = col.shape[0]
    at = lax.broadcasted_iota(jnp.int32, (size, size), 0)
    to = lax.broadcasted_iota(jnp.int32, (size, size), 1)
    hit = jnp.logical_and(jnp.abs(at - to) <= HALF, col == row)
    ones = jnp.where(hit, 1.0, 0.0).astype(F32)
    return ones.astype(BF16), jnp.sum(ones, axis=1, keepdims=True)


def call(body, name, ins, outs, scratch, flops=0, moved=0, aliases=None, limit=58):
    spaces = {"v": pltpu.VMEM, "a": pl.ANY, "s": pltpu.SMEM}
    return pl.pallas_call(
        body,
        name=name,
        out_shape=[jax.ShapeDtypeStruct(shape, kind) for shape, kind, _ in outs],
        in_specs=[pl.BlockSpec(memory_space=spaces[place]) for _, place in ins],
        out_specs=[pl.BlockSpec(memory_space=spaces[place]) for _, _, place in outs],
        scratch_shapes=scratch,
        input_output_aliases=aliases or {},
        cost_estimate=pl.CostEstimate(flops=flops, bytes_accessed=moved, transcendentals=0),
        compiler_params=pltpu.CompilerParams(vmem_limit_bytes=limit << 20),
    )(*[array for array, _ in ins])


def sems(count):
    return pltpu.SemaphoreType.DMA((count,))


class Copies:
    def __init__(self, ref):
        self.ref = ref
        self.used = 0

    def go(self, source, target):
        copy = pltpu.make_async_copy(source, target, self.ref.at[self.used])
        self.used += 1
        copy.start()
        return copy


def all_wait(copies):
    for copy in copies:
        copy.wait()


def season_body(sid, x, sc, sr, bias, w, season, down, squash, cb, wbuf, sem):
    first = sid[0] == 0
    rows = sr.shape[1]
    buffers = sr.shape[0]

    def tile_copy(k):
        return pltpu.make_async_copy(w.at[k], wbuf.at[k], sem.at[k])

    @pl.when(first)
    def _():
        for k in range(DOWN_TILES):
            tile_copy(k).start()

    for m in range(buffers):
        span = slice(m * rows, (m + 1) * rows)
        ones, count = window_of(sc[span, :], sr[m : m + 1, :])
        feed = x[span, :]
        low = (feed.astype(F32) - mm(ones, feed) / count).astype(BF16)
        season[span, :] = low
        block_set(cb, (), m * rows, rows, low.astype(F32))

    @pl.when(first)
    def _():
        at = 0
        for member in range(2):
            stride = STRIDES[member]
            spots = buffers * rows // stride
            total = jnp.zeros((spots, D), F32)
            for k in range(stride):
                tile = FIRST_TILE[member] + k
                tile_copy(tile).wait()
                total += mm(spread_get(cb, (), k, spots, stride).astype(BF16), wbuf[tile])
            flat = jnp.tanh(total + bias[member : member + 1, :])
            squash[at : at + spots, :] = flat
            down[at : at + spots, :] = flat.astype(BF16)
            at += spots


def trend_body(sid, x, cot, sc, sr, bias, w, tp, ig, dw, xv, gv, tpv, igv, dwv, wv, sem):
    rows = sr.shape[1]
    buffers = sr.shape[0]

    @pl.when(sid[0] == 3)
    def _():
        go = Copies(sem)
        all_wait([go.go(x, xv), go.go(cot, gv), go.go(w.at[2 * HIDDEN_TILES], wv)])
        total = jnp.zeros((D, D), F32)
        for m in range(buffers):
            span = slice(m * rows, (m + 1) * rows)
            ones, count = window_of(sc[span, :], sr[m : m + 1, :])
            trend = (mm(ones, xv[span, :]) / count).astype(BF16)
            target = gv[span, :]
            tpv[span, :] = mm(trend, wv[...]) + bias[6:7, :]
            total += mm_tn(trend, target)
            back = (mm_nt(target, wv[...]) / count).astype(BF16)
            igv[span, :] = mm(ones, back).astype(BF16)
        dwv[...] = total
        all_wait([go.go(tpv, tp), go.go(igv, ig), go.go(dwv, dw)])


def iso_body(sid, down, mask_a, mask_b, bias, gain, w, iso, squash, pad, wbuf, sem):
    def tile_copy(k):
        return pltpu.make_async_copy(w.at[k], wbuf.at[k], sem.at[k])

    @pl.when(sid[0] == 1)
    def _():
        for k in range(DOWN_TILES):
            tile_copy(k).start()
        at = 0
        for member, mask in enumerate((mask_a, mask_b)):
            spots = mask.shape[0]
            own = down[at : at + spots, :].astype(F32)
            pad[0:16, :] = jnp.zeros((16, D), F32)
            pad[16 : 16 + spots, :] = own
            total = jnp.zeros((spots, D), F32)
            for j in range(TAPS[member]):
                tile = FIRST_TAP[member] + j
                moved = (pad[16 - j : 16 - j + spots, :] * mask[:, j : j + 1]).astype(BF16)
                tile_copy(tile).wait()
                total += mm(moved, wbuf[tile])
            flat = jnp.tanh(total + bias[member : member + 1, :])
            squash[at : at + spots, :] = flat
            n, _ = normal(flat + own)
            out = n * gain[member : member + 1, :] + bias[2 + member : 3 + member, :]
            iso[at : at + spots, :] = out.astype(BF16)
            at += spots


def merge_body(sid, iso, season, bias, gain, w, mixed, u, up, ucb, sv, mv, uv, wbuf, sem):
    total_rows = sv.shape[0]
    step = 128

    def tile_copy(k):
        return pltpu.make_async_copy(w.at[k], wbuf.at[k], sem.at[k])

    @pl.when(sid[0] == 2)
    def _():
        for k in range(DOWN_TILES + 2):
            tile_copy(k).start()
        load = pltpu.make_async_copy(season, sv, sem.at[DOWN_TILES + 2])
        load.start()
        at = 0
        for member in range(2):
            stride = STRIDES[member]
            spots = total_rows // stride
            own = iso[at : at + spots, :]
            for k in range(stride):
                tile = FIRST_TILE[member] + k
                tile_copy(tile).wait()
                flat = jnp.tanh(mm(own, wbuf[tile]) + bias[member : member + 1, :])
                spread_set(ucb, (member,), k, spots, stride, flat)
            at += spots
        load.wait()
        tile_copy(DOWN_TILES).wait()
        tile_copy(DOWN_TILES + 1).wait()
        keep = pltpu.make_async_copy(ucb, u, sem.at[DOWN_TILES + 3])
        keep.start()
        for start in range(0, total_rows, step):
            span = slice(start, start + step)
            low = sv[span, :].astype(F32)
            total = jnp.zeros((step, D), F32) + bias[4:5, :]
            for member in range(2):
                n, _ = normal(block_get(ucb, (member,), start, step) + low)
                upward = n * gain[member : member + 1, :] + bias[2 + member : 3 + member, :]
                upward = upward.astype(BF16)
                uv[member, span, :] = upward
                total += mm(upward, wbuf[DOWN_TILES + member])
            mv[span, :] = total.astype(BF16)
        out = pltpu.make_async_copy(mv, mixed, sem.at[DOWN_TILES + 4])
        out.start()
        out_up = pltpu.make_async_copy(uv, up, sem.at[DOWN_TILES + 5])
        out_up.start()
        keep.wait()
        out.wait()
        out_up.wait()


def ffn_body(sid, mixed, cot, tp, bias, gain, w, out, gm, act, gb, dh, small,
             mv, cv, tv, wbuf, ov, gmv, av, gbv, dhv, gd, sem):
    rows = mv.shape[0]
    half = math.sqrt(0.5)
    dense = 1.0 / math.sqrt(2.0 * math.pi)

    @pl.when(sid[0] == 3)
    def _():
        go = Copies(sem)
        loads = [go.go(mixed, mv), go.go(w.at[pl.ds(0, 2 * HIDDEN_TILES)], wbuf)]
        loads += [go.go(cot, cv), go.go(tp, tv)]
        all_wait(loads)
        low = mv[...]
        branch = jnp.zeros((rows, D), F32) + bias[4:5, :]
        for k in range(HIDDEN_TILES):
            h = mm(low, wbuf[k]) + bias[k : k + 1, :]
            share = 0.5 * (1.0 + lax.erf(h * half))
            a = (h * share).astype(BF16)
            gd[k] = share + h * jnp.exp(h * h * -0.5) * dense
            av[k] = a
            branch += mm(a, wbuf[HIDDEN_TILES + k])
        n, scale = normal(low.astype(F32) + branch)
        ov[...] = (n * gain[0:1, :] + bias[5:6, :] + tv[...]).astype(BF16)
        target = cv[...].astype(F32)
        grad = normal_back(target, gain[0:1, :], n, scale)
        grad_low = grad.astype(BF16)
        gbv[...] = grad_low
        shift = col_sum(target)
        small[...] = jnp.zeros((SMALL_ROWS, D), F32)
        small[4:5, :] = col_sum(grad_low.astype(F32))
        small[5:6, :] = shift
        small[6:7, :] = shift
        small[8:9, :] = col_sum(target * n)
        for k in range(HIDDEN_TILES):
            low_k = (mm_nt(grad_low, wbuf[HIDDEN_TILES + k]) * gd[k]).astype(BF16)
            dhv[k] = low_k
            small[k : k + 1, :] = col_sum(low_k.astype(F32))
            grad += mm_nt(low_k, wbuf[k])
        gmv[...] = grad.astype(BF16)
        all_wait(
            [go.go(ov, out), go.go(gmv, gm), go.go(av, act), go.go(gbv, gb), go.go(dhv, dh)]
        )


def ffn_grad_body(count, sid, *refs):
    mixed, act, gb, dh = (refs[i * count : (i + 1) * count] for i in range(4))
    dw8, total, mv, av, gv, dv, tv, wv, sem = refs[4 * count :]

    @pl.when(sid[0] == 3)
    def _():
        go = Copies(sem)
        loads = [go.go(dw8, wv)]
        for c in range(count):
            loads += [go.go(mixed[c], mv.at[c]), go.go(act[c], av.at[c])]
            loads += [go.go(gb[c], gv.at[c]), go.go(dh[c], dv.at[c])]
        all_wait(loads)
        for k in range(HIDDEN_TILES):
            first = jnp.zeros((D, D), F32)
            second = jnp.zeros((D, D), F32)
            for c in range(count):
                first += mm_tn(mv[c], dv[c, k])
                second += mm_tn(av[c, k], gv[c])
            tv[k] = first.astype(BF16)
            tv[HIDDEN_TILES + k] = second.astype(BF16)
        tv[2 * HIDDEN_TILES] = wv[...].astype(BF16)
        go.go(tv, total).wait()


def up_grad_body(first_row, sid, gm, u, season, bias, gain, w, g, gw, small,
                 gmv, uv, sv, wv, gv, gwv, sem):
    rows = gmv.shape[0]
    step = 128

    @pl.when(sid[0] == 2)
    def _():
        go = Copies(sem)
        span = pl.ds(first_row, rows)
        all_wait(
            [
                go.go(gm, gmv),
                go.go(u.at[:, :, span, :], uv),
                go.go(season.at[span, :], sv),
                go.go(w.at[pl.ds(DOWN_TILES, 2)], wv),
            ]
        )
        small[...] = jnp.zeros((SMALL_ROWS, D), F32)
        for start in range(0, rows, step):
            part = slice(start, start + step)
            low = sv[part, :].astype(F32)
            grad_mixed = gmv[part, :]
            small[4:5, :] += col_sum(grad_mixed.astype(F32))
            wire = jnp.zeros((step, D), F32)
            for member in range(2):
                o = mm_nt(grad_mixed, wv[member])
                flat = block_get(uv, (member,), start, step)
                n, scale = normal(flat + low)
                back = normal_back(o, gain[member : member + 1, :], n, scale)
                wire += back
                cell = (back * (1.0 - flat * flat)).astype(BF16).astype(F32)
                block_set(gv, (member,), start, step, cell)
                small[member : member + 1, :] += col_sum(cell)
                small[2 + member : 3 + member, :] += col_sum(o)
                small[8 + member : 9 + member, :] += col_sum(o * n)
            gwv[part, :] = wire
        all_wait([go.go(gv, g), go.go(gwv, gw)])


def up_dx_body(count, sid, *refs):
    g = refs[:count]
    w, out, gv, wbuf, sem = refs[count:]
    total_rows = gv.shape[2]
    rows = total_rows // count

    def tile_copy(k):
        return pltpu.make_async_copy(w.at[k], wbuf.at[k], sem.at[k])

    @pl.when(sid[0] == 2)
    def _():
        loads = [
            pltpu.make_async_copy(
                g[c], gv.at[:, :, pl.ds(c * rows, rows), :], sem.at[DOWN_TILES + c]
            )
            for c in range(count)
        ]
        for load in loads:
            load.start()
        for k in range(DOWN_TILES):
            tile_copy(k).start()
        all_wait(loads)
        at = 0
        for member in range(2):
            stride = STRIDES[member]
            spots = total_rows // stride
            total = jnp.zeros((spots, D), F32)
            for k in range(stride):
                tile = FIRST_TILE[member] + k
                tile_copy(tile).wait()
                cell = spread_get(gv, (member,), k, spots, stride).astype(BF16)
                total += mm_nt(cell, wbuf[tile])
            out[at : at + spots, :] = total.astype(BF16)
            at += spots


def merge_grad_body(count, sid, *refs):
    gm = refs[:count]
    gw = refs[count : 2 * count]
    up, sc, sr, held, ig, total, gmv, gwv, upv, igv, tv, sem = refs[2 * count :]
    buffers, rows = sr.shape
    part = buffers * rows // count

    @pl.when(sid[0] == 2)
    def _():
        go = Copies(sem)
        loads = [go.go(up, upv)]
        for c in range(count):
            loads.append(go.go(gm[c], gmv.at[pl.ds(c * part, part), :]))
            loads.append(go.go(gw[c], gwv.at[pl.ds(c * part, part), :]))
        all_wait(loads)
        for member in range(2):
            tv[member] = mm_tn(upv[member], gmv[...]).astype(BF16)
        for m in range(buffers):
            span = slice(m * rows, (m + 1) * rows)
            ones, count_rows = window_of(sc[span, :], sr[m : m + 1, :])
            wire = gwv[span, :]
            away = mm(ones, (wire / count_rows).astype(BF16))
            igv[span, :] = (wire - away).astype(BF16)
        all_wait([go.go(tv, total.at[pl.ds(0, 2)]), go.go(igv, ig)])


def iso_grad_body(sid, grad, down, squash, back_a, back_b, bias, gain, w, gq, gdown, small,
                  pad, wbuf, sem):
    def tile_copy(k):
        return pltpu.make_async_copy(w.at[k], wbuf.at[k], sem.at[k])

    @pl.when(sid[0] == 1)
    def _():
        for k in range(DOWN_TILES):
            tile_copy(k).start()
        small[...] = jnp.zeros((SMALL_ROWS, D), F32)
        at = 0
        for member, mask in enumerate((back_a, back_b)):
            spots = mask.shape[0]
            span = slice(at, at + spots)
            flat = squash[span, :]
            n, scale = normal(flat + down[span, :].astype(F32))
            o = grad[span, :].astype(F32)
            total = normal_back(o, gain[member : member + 1, :], n, scale)
            cell = (total * (1.0 - flat * flat)).astype(BF16)
            gq[span, :] = cell
            wide = cell.astype(F32)
            small[member : member + 1, :] = col_sum(wide)
            small[2 + member : 3 + member, :] = col_sum(o)
            small[8 + member : 9 + member, :] = col_sum(o * n)
            pad[0:spots, :] = wide
            pad[spots : spots + 16, :] = jnp.zeros((16, D), F32)
            for j in range(TAPS[member]):
                tile = FIRST_TAP[member] + j
                moved = (pad[j : j + spots, :] * mask[:, j : j + 1]).astype(BF16)
                tile_copy(tile).wait()
                total += mm_nt(moved, wbuf[tile])
            gdown[span, :] = total.astype(BF16)
            at += spots


def payload_body(sid, gdown, squash, gq, small_1, small_2, small_3, out):
    spots = gdown.shape[0]

    def put_small(value):
        high = value.astype(BF16)
        out[spots : spots + SMALL_ROWS, :] = high
        out[spots + SMALL_ROWS : spots + 2 * SMALL_ROWS, :] = (value - high.astype(F32)).astype(
            BF16
        )

    @pl.when(sid[0] == 0)
    def _():
        flat = squash[...]
        cell = (gdown[...].astype(F32) * (1.0 - flat * flat)).astype(BF16)
        out[0:spots, :] = cell
        wide = cell.astype(F32)
        cut = (spots // 7) * 4
        rows = lax.broadcasted_iota(jnp.int32, (SMALL_ROWS, D), 0)
        value = jnp.where(rows == 0, col_sum(wide[:cut, :]), 0.0)
        value = jnp.where(rows == 1, col_sum(wide[cut:, :]), value)
        put_small(value)

    @pl.when(sid[0] == 1)
    def _():
        out[0:spots, :] = gq[...]
        put_small(small_1[...])

    @pl.when(sid[0] == 2)
    def _():
        out[0:spots, :] = jnp.zeros((spots, D), BF16)
        put_small(small_2[...])

    @pl.when(sid[0] == 3)
    def _():
        out[0:spots, :] = jnp.zeros((spots, D), BF16)
        put_small(small_3[...])


def feed_grad_body(sid, gp, ig_2, ig_3, sc, sr, w, ig, cb, igv, wbuf, sem):
    buffers, rows = sr.shape
    total_rows = buffers * rows

    def tile_copy(k):
        return pltpu.make_async_copy(w.at[k], wbuf.at[k], sem.at[k])

    @pl.when(sid[0] == 0)
    def _():
        for k in range(DOWN_TILES):
            tile_copy(k).start()
        at = 0
        for member in range(2):
            stride = STRIDES[member]
            spots = total_rows // stride
            cell = gp[at : at + spots, :]
            for k in range(stride):
                tile = FIRST_TILE[member] + k
                tile_copy(tile).wait()
                back = mm_nt(cell, wbuf[tile])
                if member == 1:
                    back += spread_get(cb, (), k, spots, stride)
                spread_set(cb, (), k, spots, stride, back)
            at += spots
        for m in range(buffers):
            span = slice(m * rows, (m + 1) * rows)
            ones, count = window_of(sc[span, :], sr[m : m + 1, :])
            season = block_get(cb, (), m * rows, rows)
            igv[span, :] = (season - mm(ones, (season / count).astype(BF16))).astype(BF16)
        copy = pltpu.make_async_copy(igv, ig, sem.at[DOWN_TILES])
        copy.start()
        copy.wait()

    @pl.when(sid[0] == 1)
    def _():
        igv[...] = jnp.zeros(igv.shape, BF16)
        copy = pltpu.make_async_copy(igv, ig, sem.at[DOWN_TILES])
        copy.start()
        copy.wait()

    @pl.when(sid[0] == 2)
    def _():
        copy = pltpu.make_async_copy(ig_2, ig, sem.at[DOWN_TILES])
        copy.start()
        copy.wait()

    @pl.when(sid[0] == 3)
    def _():
        copy = pltpu.make_async_copy(ig_3, ig, sem.at[DOWN_TILES])
        copy.start()
        copy.wait()


def season_flip_body(sid, season, out_a, out_b, sv, cb, st_a, st_b, sem):
    rows = sv.shape[0]
    groups = season.shape[0] // rows

    @pl.when(sid[0] == 0)
    def _():
        def group(i, carry):
            load = pltpu.make_async_copy(season.at[pl.ds(i * rows, rows), :], sv, sem.at[0])
            load.start()
            load.wait()

            def widen(r, inner):
                at = pl.multiple_of(r * 256, 256)
                block_set(cb, (), at, 256, sv[pl.ds(at, 256), :].astype(F32))
                return inner

            lax.fori_loop(0, rows // 256, widen, 0)
            for member, stage in enumerate((st_a, st_b)):
                stride = STRIDES[member]
                spots = rows // stride

                def flip(k, inner, stage=stage, stride=stride, spots=spots):
                    stage[k] = spread_get(cb, (), k, spots, stride).T.astype(BF16)
                    return inner

                lax.fori_loop(0, stride, flip, 0)
            spots_a, spots_b = rows // SCALE_A, rows // SCALE_B
            copies = [
                pltpu.make_async_copy(
                    st_a, out_a.at[:, :, pl.ds(pl.multiple_of(i * spots_a, 128), spots_a)], sem.at[1]
                ),
                pltpu.make_async_copy(
                    st_b, out_b.at[:, :, pl.ds(pl.multiple_of(i * spots_b, 128), spots_b)], sem.at[2]
                ),
            ]
            for copy in copies:
                copy.start()
            all_wait(copies)
            return carry

        lax.fori_loop(0, groups, group, 0)


def up_grad_all_body(sid, gm, season, iso, bias, gain, w, out_a, out_b,
                     gmv, sv, isov, cb, ocb, st_a, st_b, wbuf, sem):
    rows = gmv.shape[0]
    blocks = gm.shape[0]
    step = 256

    @pl.when(sid[0] == 2)
    def _():
        load = pltpu.make_async_copy(w, wbuf, sem.at[0])
        load.start()
        load.wait()

        def block(i, carry):
            go = Copies(sem)
            all_wait(
                [
                    go.go(gm.at[i], gmv),
                    go.go(season.at[pl.ds(pl.multiple_of(i * rows, 128), rows), :], sv),
                    go.go(iso.at[i], isov),
                ]
            )

            def widen(r, inner):
                at = pl.multiple_of(r * step, step)
                block_set(cb, (), at, step, sv[pl.ds(at, step), :].astype(F32))
                for member in range(2):
                    o = mm_nt(gmv[pl.ds(at, step), :], wbuf[DOWN_TILES + member])
                    block_set(ocb, (member,), at, step, o)
                return inner

            lax.fori_loop(0, rows // step, widen, 0)
            at = 0
            for member, stage in enumerate((st_a, st_b)):
                stride = STRIDES[member]
                spots = rows // stride

                def tile(k, inner, stage=stage, stride=stride, spots=spots, at=at, member=member):
                    own = isov[at : at + spots, :]
                    flat = mm(own, wbuf[FIRST_TILE[member] + k]) + bias[member : member + 1, :]
                    flat = jnp.tanh(flat)
                    n, scale = normal(flat + spread_get(cb, (), k, spots, stride))
                    o = spread_get(ocb, (member,), k, spots, stride)
                    back = normal_back(o, gain[member : member + 1, :], n, scale)
                    stage[k] = (back * (1.0 - flat * flat)).astype(BF16)
                    return inner

                lax.fori_loop(0, stride, tile, 0)
                at += spots
            spots_a, spots_b = rows // SCALE_A, rows // SCALE_B
            all_wait(
                [
                    go.go(st_a, out_a.at[:, pl.ds(pl.multiple_of(i * spots_a, 32), spots_a), :]),
                    go.go(st_b, out_b.at[:, pl.ds(pl.multiple_of(i * spots_b, 32), spots_b), :]),
                ]
            )
            return carry

        lax.fori_loop(0, blocks, block, 0)


def tile_grad_body(sid, pay_1, pay_2, flip_a, flip_b, cell_a, cell_b, art, back_a, back_b,
                   tiles, bias_out, gain_out,
                   flat, turned, left, right, stage, sv, sem):
    blocks = pay_1.shape[0]
    spots_of = (back_a.shape[0] // blocks, back_b.shape[0] // blocks)
    first_spot = (0, spots_of[0])
    spots_all = spots_of[0] + spots_of[1]
    per = 8
    groups = blocks // per
    lead = sid[0]

    def out_copy(tile, slot):
        return pltpu.make_async_copy(stage.at[slot], tiles.at[tile], sem.at[slot])

    all_small = [
        pltpu.make_async_copy(pay_2.at[i, pl.ds(spots_all, 2 * SMALL_ROWS), :], sv.at[i], sem.at[8])
        for i in range(blocks)
    ]
    for copy in all_small:
        copy.start()
        copy.wait()
    summed = jnp.zeros((SMALL_ROWS, D), F32)
    for i in range(blocks):
        summed += sv[i, 0:SMALL_ROWS, :].astype(F32) + sv[i, SMALL_ROWS:, :].astype(F32)
    bias_out[...] = summed[0:7, :]
    gain_out[...] = summed[8:10, :]

    def run(member, count, first_out, source, operand):
        spots = per * spots_of[member]
        steps = count * groups

        def fetch(t, slot):
            k, g = t // groups, t % groups
            at = pl.multiple_of(g * spots, 256)
            if source == "left":
                ref = (flip_a, flip_b)[member]
                return pltpu.make_async_copy(
                    ref.at[k, :, pl.ds(at, spots)], left.at[slot, :, pl.ds(0, spots)], sem.at[4 + slot]
                )
            ref = (cell_a, cell_b)[member]
            return pltpu.make_async_copy(
                ref.at[k, pl.ds(at, spots), :], right.at[slot, pl.ds(0, spots), :], sem.at[4 + slot]
            )

        if source:
            fetch(0, 0).start()

        def step(t, carry):
            slot = t % 2
            k, g = t // groups, t % groups
            if source:

                @pl.when(t + 1 < steps)
                def _():
                    fetch(t + 1, 1 - slot).start()

                fetch(t, slot).wait()
            out_slot = k % 2

            @pl.when(jnp.logical_and(g == 0, k >= 2))
            def _():
                out_copy(first_out + k - 2, out_slot).wait()

            value = operand(k, g, slot, spots)

            @pl.when(g == 0)
            def _():
                stage[out_slot] = value

            @pl.when(g > 0)
            def _():
                stage[out_slot] += value

            @pl.when(g == groups - 1)
            def _():
                out_copy(first_out + k, out_slot).start()

            return carry

        lax.fori_loop(0, steps, step, 0)
        out_copy(first_out + count - 2, (count - 2) % 2).wait()
        out_copy(first_out + count - 1, (count - 1) % 2).wait()

    def take(pay, member):
        spots = spots_of[member]
        copies = [
            pltpu.make_async_copy(
                pay.at[i, pl.ds(first_spot[member], spots), :],
                flat.at[pl.ds(i * spots, spots), :],
                sem.at[8],
            )
            for i in range(blocks)
        ]
        for copy in copies:
            copy.start()
            copy.wait()

    def turn(member):
        spots = per * spots_of[member]

        def one(g, carry):
            at = pl.multiple_of(g * spots, 256)
            turned[:, pl.ds(at, spots)] = flat[pl.ds(at, spots), :].astype(F32).T.astype(BF16)
            return carry

        lax.fori_loop(0, groups, one, 0)

    def blank(first, last):
        stage[0] = jnp.zeros((D, D), F32)
        for tile in range(first, last):
            out_copy(tile, 0).start()
            out_copy(tile, 0).wait()

    @pl.when(lead == 0)
    def _():
        for member in range(2):
            take(pay_2, member)

            def operand(k, g, slot, spots):
                at = pl.multiple_of(g * spots, 256)
                return mm(left[slot, :, 0:spots], flat[pl.ds(at, spots), :])

            run(member, STRIDES[member], FIRST_TILE[member], "left", operand)
        blank(DOWN_TILES, tiles.shape[0])

    @pl.when(lead == 1)
    def _():
        for member in range(2):
            take(pay_1, member)
            turn(member)
            take(pay_2, member)
            mask = (back_a, back_b)[member]

            def operand(k, g, slot, spots, mask=mask):
                at = pl.multiple_of(g * spots, 256)
                wide = jnp.concatenate(
                    [flat[pl.ds(at, spots), :].astype(F32)], 0
                )
                moved = pltpu.roll(wide, lax.rem(spots - k, spots), 0)
                lane = lax.broadcasted_iota(jnp.int32, (spots, mask.shape[1]), 1)
                hit = jnp.sum(
                    jnp.where(lane == k, mask[pl.ds(at, spots), :], 0.0), axis=1, keepdims=True
                )
                return mm(turned[:, pl.ds(at, spots)], (moved * hit).astype(BF16))

            run(member, TAPS[member], FIRST_TAP[member], "", operand)
        blank(DOWN_TILES, tiles.shape[0])

    @pl.when(lead == 2)
    def _():
        for member in range(2):
            take(pay_1, member)
            turn(member)

            def operand(k, g, slot, spots):
                at = pl.multiple_of(g * spots, 256)
                return mm(turned[:, pl.ds(at, spots)], right[slot, 0:spots, :])

            run(member, STRIDES[member], FIRST_TILE[member], "right", operand)
        for member in range(2):
            load = pltpu.make_async_copy(art.at[member], right.at[0, pl.ds(0, D), :], sem.at[8])
            load.start()
            load.wait()
            stage[0] = right[0, 0:D, :].astype(F32)
            out_copy(DOWN_TILES + member, 0).start()
            out_copy(DOWN_TILES + member, 0).wait()

    @pl.when(lead == 3)
    def _():
        for k in range(2 * HIDDEN_TILES + 1):
            load = pltpu.make_async_copy(art.at[k], right.at[0, pl.ds(0, D), :], sem.at[8])
            load.start()
            load.wait()
            stage[0] = right[0, 0:D, :].astype(F32)
            out_copy(k, 0).start()
            out_copy(k, 0).wait()
        blank(2 * HIDDEN_TILES + 1, tiles.shape[0])


def shifted_masks(spot_series, taps, forward):
    buffers, spots = spot_series.shape
    fill = jnp.full((buffers, taps), -1, spot_series.dtype)
    if forward:
        padded = jnp.concatenate([fill, spot_series], 1)
        moved = [padded[:, taps - j : taps - j + spots] for j in range(taps)]
    else:
        padded = jnp.concatenate([spot_series, fill], 1)
        moved = [padded[:, j : j + spots] for j in range(taps)]
    hits = [(part == spot_series).astype(F32) for part in moved]
    return jnp.stack(hits, 2).reshape(buffers * spots, taps)


def shards(inputs, weights, biases, gain_rows, block_series, cotangent):
    section = lax.axis_index("section")
    sections = lax.axis_size("section")
    dp = lax.axis_size("dp")
    buffers = block_series.shape[0]
    total_rows = inputs.shape[0]
    rows = total_rows // buffers
    tile_count = weights.shape[0]
    spots_a, spots_b = total_rows // SCALE_A, total_rows // SCALE_B
    spots = spots_a + spots_b
    sid = section.astype(jnp.int32).reshape(1)
    row_series = jnp.repeat(block_series, BLOCK, axis=1)
    sc = row_series.reshape(total_rows, 1)
    sr = row_series
    spot_series_a = jnp.repeat(block_series, BLOCK // SCALE_A, axis=1)
    spot_series_b = jnp.repeat(block_series, BLOCK // SCALE_B, axis=1)
    tile = (D, D)

    def permute(value, source, target):
        return lax.ppermute(value, "section", [(source, target)])

    season, down, squash_0 = call(
        season_body,
        "season",
        [(sid, "s"), (inputs, "v"), (sc, "v"), (sr, "v"), (biases, "v"), (weights, "a")],
        [((total_rows, D), BF16, "v"), ((spots, D), BF16, "v"), ((spots, D), F32, "v")],
        [
            pltpu.VMEM((COLS, total_rows, LANES), F32),
            pltpu.VMEM((DOWN_TILES,) + tile, BF16),
            sems(DOWN_TILES),
        ],
        flops=4 * 10**9,
        moved=20 * 10**6,
    )
    down_in = permute(down, 0, 1)
    season_all = lax.all_gather(season, "dp", axis=0, tiled=True)
    tp, ig_3, dw8 = call(
        trend_body,
        "trend",
        [(sid, "s"), (inputs, "a"), (cotangent, "a"), (sc, "v"), (sr, "v"), (biases, "v"),
         (weights, "a")],
        [((total_rows, D), F32, "a"), ((total_rows, D), BF16, "a"), (tile, F32, "a")],
        [
            pltpu.VMEM((total_rows, D), BF16),
            pltpu.VMEM((total_rows, D), BF16),
            pltpu.VMEM((total_rows, D), F32),
            pltpu.VMEM((total_rows, D), BF16),
            pltpu.VMEM(tile, F32),
            pltpu.VMEM(tile, BF16),
            sems(6),
        ],
        flops=5 * 10**9,
        moved=10 * 10**6,
    )
    iso, squash_1 = call(
        iso_body,
        "iso",
        [(sid, "s"), (down_in, "v"), (shifted_masks(spot_series_a, TAPS_A, True), "v"),
         (shifted_masks(spot_series_b, TAPS_B, True), "v"), (biases, "v"), (gain_rows, "v"),
         (weights, "a")],
        [((spots, D), BF16, "v"), ((spots, D), F32, "v")],
        [
            pltpu.VMEM((16 + spots_a, D), F32),
            pltpu.VMEM((DOWN_TILES,) + tile, BF16),
            sems(DOWN_TILES),
        ],
        flops=2 * 10**9,
        moved=15 * 10**6,
    )
    iso_in = permute(iso, 1, 2)
    spread = jnp.where(section == 1, down_in, iso_in)
    numbers = jnp.zeros((SMALL_ROWS, D), BF16)
    numbers = numbers.at[0, :spots_a].set(spot_series_a.reshape(-1).astype(BF16))
    numbers = numbers.at[1, :spots_b].set(spot_series_b.reshape(-1).astype(BF16))
    pay_1 = lax.all_gather(jnp.concatenate([spread, numbers], 0), "dp", axis=0, tiled=False)
    mixed, u, up = call(
        merge_body,
        "merge",
        [(sid, "s"), (iso_in, "v"), (season, "a"), (biases, "v"), (gain_rows, "v"), (weights, "a")],
        [((total_rows, D), BF16, "a"), ((2, COLS, total_rows, LANES), F32, "a"),
         ((2, total_rows, D), BF16, "a")],
        [
            pltpu.VMEM((2, COLS, total_rows, LANES), F32),
            pltpu.VMEM((total_rows, D), BF16),
            pltpu.VMEM((total_rows, D), BF16),
            pltpu.VMEM((2, total_rows, D), BF16),
            pltpu.VMEM((DOWN_TILES + 2,) + tile, BF16),
            sems(DOWN_TILES + 6),
        ],
        flops=4 * 10**9,
        moved=25 * 10**6,
    )

    def ffn(mixed_part, first):
        part = mixed_part.shape[0]
        span = slice(first, first + part)
        return call(
            ffn_body,
            "ffn",
            [(sid, "s"), (mixed_part, "a"), (cotangent[span], "a"), (tp[span], "a"), (biases, "v"),
             (gain_rows, "v"), (weights, "a")],
            [((part, D), BF16, "a"), ((part, D), BF16, "a"), ((HIDDEN_TILES, part, D), BF16, "a"),
             ((part, D), BF16, "a"), ((HIDDEN_TILES, part, D), BF16, "a"),
             ((SMALL_ROWS, D), F32, "v")],
            [
                pltpu.VMEM((part, D), BF16),
                pltpu.VMEM((part, D), BF16),
                pltpu.VMEM((part, D), F32),
                pltpu.VMEM((2 * HIDDEN_TILES,) + tile, BF16),
                pltpu.VMEM((part, D), BF16),
                pltpu.VMEM((part, D), BF16),
                pltpu.VMEM((HIDDEN_TILES, part, D), BF16),
                pltpu.VMEM((part, D), BF16),
                pltpu.VMEM((HIDDEN_TILES, part, D), BF16),
                pltpu.VMEM((HIDDEN_TILES, part, D), F32),
                sems(10),
            ],
            flops=6 * part * D * 4 * D * 2,
            moved=20 * 10**6,
        )

    count = buffers
    mixed_in, results = [], []
    for c in range(count):
        part = permute(mixed[c * rows : (c + 1) * rows], 2, 3)
        mixed_in.append(part)
        results.append(ffn(part, c * rows))
    small_3 = sum(r[5] for r in results)
    gm_in = [permute(r[1], 3, 2) for r in results]
    art = call(
        lambda *refs: ffn_grad_body(count, *refs),
        "ffn_grad",
        [(sid, "s")]
        + [(part, "a") for part in mixed_in]
        + [(r[2], "a") for r in results]
        + [(r[3], "a") for r in results]
        + [(r[4], "a") for r in results]
        + [(dw8, "a")],
        [((2 * HIDDEN_TILES + 1,) + tile, BF16, "a")],
        [
            pltpu.VMEM((count, rows, D), BF16),
            pltpu.VMEM((count, HIDDEN_TILES, rows, D), BF16),
            pltpu.VMEM((count, rows, D), BF16),
            pltpu.VMEM((count, HIDDEN_TILES, rows, D), BF16),
            pltpu.VMEM((2 * HIDDEN_TILES + 1,) + tile, BF16),
            pltpu.VMEM(tile, F32),
            sems(4 * count + 2),
        ],
        flops=16 * total_rows * D * D,
        moved=25 * 10**6,
    )[0]
    ups = []
    for c in range(count):
        ups.append(
            call(
                lambda *refs, c=c: up_grad_body(c * rows, *refs),
                "up_grad",
                [(sid, "s"), (gm_in[c], "a"), (u, "a"), (season, "a"), (biases, "v"),
                 (gain_rows, "v"), (weights, "a")],
                [((2, COLS, rows, LANES), F32, "a"), ((rows, D), F32, "a"),
                 ((SMALL_ROWS, D), F32, "v")],
                [
                    pltpu.VMEM((rows, D), BF16),
                    pltpu.VMEM((2, COLS, rows, LANES), F32),
                    pltpu.VMEM((rows, D), BF16),
                    pltpu.VMEM((2,) + tile, BF16),
                    pltpu.VMEM((2, COLS, rows, LANES), F32),
                    pltpu.VMEM((rows, D), F32),
                    sems(6),
                ],
                flops=2 * 10**9,
                moved=6 * 10**6,
            )
        )
    small_2 = sum(r[2] for r in ups)
    giso = call(
        lambda *refs: up_dx_body(count, *refs),
        "up_dx",
        [(sid, "s")] + [(r[0], "a") for r in ups] + [(weights, "a")],
        [((spots, D), BF16, "v")],
        [
            pltpu.VMEM((2, COLS, total_rows, LANES), F32),
            pltpu.VMEM((DOWN_TILES,) + tile, BF16),
            sems(DOWN_TILES + count),
        ],
        flops=2 * 10**9,
        moved=20 * 10**6,
    )[0]
    giso_in = permute(giso, 2, 1)
    gm_all = lax.all_gather(jnp.concatenate(gm_in, 0), "dp", axis=0, tiled=False)
    ig_2, art = call(
        lambda *refs: merge_grad_body(count, *refs),
        "merge_grad",
        [(sid, "s")]
        + [(part, "a") for part in gm_in]
        + [(r[1], "a") for r in ups]
        + [(up, "a"), (sc, "v"), (sr, "v"), (art, "a")],
        [((total_rows, D), BF16, "a"), (art.shape, BF16, "a")],
        [
            pltpu.VMEM((total_rows, D), BF16),
            pltpu.VMEM((total_rows, D), F32),
            pltpu.VMEM((2, total_rows, D), BF16),
            pltpu.VMEM((total_rows, D), BF16),
            pltpu.VMEM((2,) + tile, BF16),
            sems(2 * count + 3),
        ],
        flops=4 * 10**9,
        moved=15 * 10**6,
        aliases={2 * count + 4: 1},
    )
    art = lax.psum(art, "dp")
    gq, gdown, small_1 = call(
        iso_grad_body,
        "iso_grad",
        [(sid, "s"), (giso_in, "v"), (down_in, "v"), (squash_1, "v"),
         (shifted_masks(spot_series_a, TAPS_A, False), "v"),
         (shifted_masks(spot_series_b, TAPS_B, False), "v"),
         (biases, "v"), (gain_rows, "v"), (weights, "a")],
        [((spots, D), BF16, "v"), ((spots, D), BF16, "v"), ((SMALL_ROWS, D), F32, "v")],
        [
            pltpu.VMEM((16 + spots_a, D), F32),
            pltpu.VMEM((DOWN_TILES,) + tile, BF16),
            sems(DOWN_TILES),
        ],
        flops=2 * 10**9,
        moved=15 * 10**6,
    )
    gdown_in = permute(gdown, 1, 0)
    payload = call(
        payload_body,
        "payload",
        [(sid, "s"), (gdown_in, "v"), (squash_0, "v"), (gq, "v"), (small_1, "v"), (small_2, "v"),
         (small_3, "v")],
        [((spots + 2 * SMALL_ROWS, D), BF16, "v")],
        [],
        moved=10**6,
    )[0]
    pay_2 = lax.all_gather(payload, "dp", axis=0, tiled=False)
    ig = call(
        feed_grad_body,
        "feed_grad",
        [(sid, "s"), (payload, "v"), (ig_2, "a"), (ig_3, "a"), (sc, "v"), (sr, "v"), (weights, "a")],
        [((total_rows, D), BF16, "a")],
        [
            pltpu.VMEM((COLS, total_rows, LANES), F32),
            pltpu.VMEM((total_rows, D), BF16),
            pltpu.VMEM((DOWN_TILES,) + tile, BF16),
            sems(DOWN_TILES + 1),
        ],
        flops=2 * 10**9,
        moved=20 * 10**6,
    )[0]
    ig = lax.psum_scatter(ig, "section", scatter_dimension=1, tiled=True)
    group = 4 * total_rows
    flip_a, flip_b = call(
        season_flip_body,
        "season_flip",
        [(sid, "s"), (season_all, "a")],
        [((SCALE_A, D, dp * spots_a), BF16, "a"), ((SCALE_B, D, dp * spots_b), BF16, "a")],
        [
            pltpu.VMEM((group, D), BF16),
            pltpu.VMEM((COLS, group, LANES), F32),
            pltpu.VMEM((SCALE_A, D, group // SCALE_A), BF16),
            pltpu.VMEM((SCALE_B, D, group // SCALE_B), BF16),
            sems(3),
        ],
        flops=10**9,
        moved=40 * 10**6,
    )
    cell_a, cell_b = call(
        up_grad_all_body,
        "up_grad_all",
        [(sid, "s"), (gm_all, "a"), (season_all, "a"), (pay_1, "a"), (biases, "v"),
         (gain_rows, "v"), (weights, "a")],
        [((SCALE_A, dp * spots_a, D), BF16, "a"), ((SCALE_B, dp * spots_b, D), BF16, "a")],
        [
            pltpu.VMEM((total_rows, D), BF16),
            pltpu.VMEM((total_rows, D), BF16),
            pltpu.VMEM((spots + SMALL_ROWS, D), BF16),
            pltpu.VMEM((COLS, total_rows, LANES), F32),
            pltpu.VMEM((2, COLS, total_rows, LANES), F32),
            pltpu.VMEM((SCALE_A, spots_a, D), BF16),
            pltpu.VMEM((SCALE_B, spots_b, D), BF16),
            pltpu.VMEM((tile_count,) + tile, BF16),
            sems(6),
        ],
        flops=25 * 10**9,
        moved=60 * 10**6,
    )
    number_a = pay_1[:, spots, :spots_a].astype(jnp.int32).reshape(dp * buffers, rows // SCALE_A)
    number_b = pay_1[:, spots + 1, :spots_b].astype(jnp.int32).reshape(dp * buffers, rows // SCALE_B)
    per = 8
    tiles, bias_grad, gain_grad = call(
        tile_grad_body,
        "tile_grad",
        [(sid, "s"), (pay_1, "a"), (pay_2, "a"), (flip_a, "a"), (flip_b, "a"), (cell_a, "a"),
         (cell_b, "a"), (art, "a"), (shifted_masks(number_a, TAPS_A, False), "v"),
         (shifted_masks(number_b, TAPS_B, False), "v")],
        [((tile_count,) + tile, F32, "a"), ((7, D), F32, "v"), ((2, D), F32, "v")],
        [
            pltpu.VMEM((dp * spots_a, D), BF16),
            pltpu.VMEM((D, dp * spots_a), BF16),
            pltpu.VMEM((2, D, per * spots_a), BF16),
            pltpu.VMEM((2, per * spots_a, D), BF16),
            pltpu.VMEM((2,) + tile, F32),
            pltpu.VMEM((dp, 2 * SMALL_ROWS, D), BF16),
            sems(9),
        ],
        flops=13 * 10**9,
        moved=60 * 10**6,
    )
    width = D // sections
    layer = jnp.concatenate([r[0] for r in results], 0)
    shares = [layer[:, j * width : (j + 1) * width] for j in range(sections)]
    own = jnp.where(section == sections - 1, shares[-1], jnp.zeros((), BF16))
    for j in range(sections - 1):
        own += permute(shares[j], sections - 1, j)
    return own, ig.astype(F32), tiles, bias_grad, gain_grad


def solution(mesh):
    return jax.shard_map(
        shards,
        mesh=mesh,
        in_specs=(
            P("dp", None),
            P("section", None, None),
            P("section", None),
            P("section", None),
            P("dp", None),
            P("dp", None),
        ),
        out_specs=(
            P("dp", "section"),
            P("dp", "section"),
            P("section", None, None),
            P("section", None),
            P("section", None),
        ),
        check_vma=False,
    )
```
